1024 devices in a mesh: dp: 16 (over z), ctx: 8 (over x, core), tp: 8 (over y).
Axes of the slice: x: 4, y: 8, z: 16, core: 2. Of those that a mesh axis runs over, the one named last changes fastest.
Arguments:
- tokens: bfloat16 [4096, 4096], P(('dp', 'ctx', 'tp')), may hold values from -24 to 24
- out_grad: bfloat16 [4096, 4096], P(('dp', 'ctx', 'tp')), may hold values from -6 to 6
- expert_ids: int32 [4096, 2], P(('dp', 'ctx', 'tp')), may hold values from 0 to 7, all different within a row; in each aligned block of 4 rows (0 to 3, 4 to 7, ...) at most 2 rows name the same one
- gates: bfloat16 [4096, 2], P(('dp', 'ctx', 'tp')), may hold values from 0.25 to 1
- gate_proj: bfloat16 [8, 1536, 4096], P('ctx', 'tp'), may hold values from -0.09375 to 0.09375
- up_proj: bfloat16 [8, 1536, 4096], P('ctx', 'tp'), may hold values from -0.09375 to 0.09375
- down_proj: bfloat16 [8, 1536, 4096], P('ctx', 'tp'), may hold values from -0.15625 to 0.15625
Outputs:
- token_grad: bfloat16 [4096, 4096], P(('dp', 'ctx', 'tp'))
- gate_proj_grad: float32 [8, 1536, 4096], P('ctx', 'tp', 'dp')
- up_proj_grad: float32 [8, 1536, 4096], P('ctx', 'tp', 'dp')
- down_proj_grad: float32 [8, 1536, 4096], P('ctx', 'tp', 'dp')
The draws below stay inside these ranges and needn't reach their ends.
Inputs may be any that keep to these rules, and one draw needn't show every extreme that they name: `expert_ids`: each token names 2 different experts. Among the 4 tokens of one device (aligned blocks of rows) no expert is named more than 2 times, and that bound is reached in every draw.
All inputs are finite; a program needn't handle non-finite values.
Results may differ from the reference program's by a relative error of at most 0.02.
Values may be sent and summed in bfloat16 or wider, within the bound.
A program may use at most 32 MiB of HBM per device.

```python
import math
import jax
import jax.numpy as jnp
import numpy as np
from jax import lax

D = 4096
FF = 1536
TOP = 2
TOK_DEV = 4
EXPERTS = 8
CAP = 2
TOKENS = 4096
N_DP = 16
N_TP = 8


def raised(array, key, source, target, blocks, factor):
    def block_of(axis_at):
        return (jnp.arange(array.shape[axis_at]) // (array.shape[axis_at] // blocks)).reshape((-1,) + (1,) * (array.ndim - 1 - axis_at))

    first = jax.random.permutation(key, blocks)[block_of(target)]
    far = (block_of(target) + blocks // 2) % blocks
    return jnp.where((block_of(source) == first) | (block_of(source) == far), factor * array, array)


def block_levels(rng, shape, shards, smallest, high):
    gain, own = 1.0, jax.random.fold_in(rng, 6)
    for dim, blocks in shards:
        draws = jnp.exp(jax.random.uniform(jax.random.fold_in(own, dim), (blocks,), jnp.float32, smallest / len(shards), high / len(shards)))
        gain = gain * jnp.repeat(draws, shape[dim] // blocks).reshape([-1 if axis == dim else 1 for axis in range(len(shape))])
    return gain


def routed_block(stream_key, own, number, rows, number_of, top, bound, skew):
    order = jax.random.permutation(stream_key, number_of)
    crowded, common = load_shares(number_of, rows * top, bound, skew, True), load_shares(number_of, rows * top, bound, skew, False)
    places = jnp.arange(number_of)

    def named(sizes, offset_by):
        used = int((sizes > 0).sum())
        fixed = max(1, used // 4)
        moved = fixed + (places - fixed + offset_by * (used - fixed)) % max(1, number_of - fixed)
        return jnp.zeros((number_of,), jnp.int32).at[order[jnp.where(places < fixed, places, moved)]].set(jnp.asarray(sizes, jnp.int32))

    sizes = jnp.where(number % 4 == 0, named(crowded, number // 4), named(common, number - number // 4 - 1))
    mixed = jax.random.permutation(jax.random.fold_in(own, 3), number_of)
    source_of, taker = mixed[0:number_of // 2 * 2:2], mixed[1:number_of // 2 * 2:2]
    slack = jnp.minimum(sizes[source_of] - 1, bound - sizes[taker]) // 2
    slack = jnp.where((source_of == order[0]) | (taker == order[0]) | (sizes[taker] == 0), 0, jnp.maximum(slack, 0))
    moved = jax.random.randint(jax.random.fold_in(own, 4), (number_of // 2,), 0, 1 << 20) % (slack + 1)
    sizes = sizes.at[source_of].add(-moved).at[taker].add(moved)
    items = jnp.searchsorted(jnp.cumsum(sizes), jnp.arange(rows * top), side="right").astype(jnp.int32)
    grid = items.reshape(top, rows).T
    grid = grid[jax.random.permutation(jax.random.fold_in(own, 1), rows)]
    offset_by = jax.random.randint(jax.random.fold_in(own, 2), (rows, 1), 0, top)
    return jnp.take_along_axis(grid, (jnp.arange(top)[None, :] + offset_by) % top, axis=1)


def load_shares(number_of, total, bound, lean, full):
    loads = [(1 << 20) // math.isqrt(standing ** lean) + 1 for standing in range(1, number_of + 1)]
    largest = bound if full else min(bound, max(-(-total // number_of), total * loads[0] // sum(loads)))
    least = 1 if total - largest >= number_of - 1 else 0
    counts, spare = [largest] + [least] * (number_of - 1), total - largest - least * (number_of - 1)
    while spare > 0:
        movable = [i for i in range(1, number_of) if counts[i] < largest] or [i for i in range(1, number_of) if counts[i] < bound]
        pool, left = sum([loads[i] for i in movable]), spare
        for i in movable:
            more = min(bound - counts[i], max(1, left * loads[i] // pool), spare)
            counts[i] = counts[i] + more
            spare = spare - more
    return np.array(counts)


def normal_values(own_key, extent, deviation, reach, pieces=(), kind=jnp.bfloat16):
    drawn = jax.random.normal(own_key, extent, jnp.float32) * deviation
    if len(pieces) > 0:
        drawn = block_levels(own_key, extent, pieces, -0.22, 0.18) * drawn
    return jnp.clip(drawn, min=-reach, max=reach).astype(kind)


def heavy_noise(key, shape, scale, limit, split, heavy, kind=jnp.bfloat16):
    values = scale * jax.random.normal(key, shape, jnp.float32)
    if split:
        values = values * block_levels(key, shape, split, -0.22, 0.18)
    return jnp.clip(raised(values, jax.random.fold_in(key, 3), *heavy), -limit, limit).astype(kind)


def setup_inputs(seed: int = 0) -> dict:
    arg_keys = jax.random.split(jax.random.key(seed), 8)
    tokens = heavy_noise(arg_keys[0], (TOKENS, D), 1.0, 24.0, ((0, 1024),), (0, 1, 1024, 6.0))
    out_grad = normal_values(arg_keys[1], (TOKENS, D), 1.0, 6.0, ((0, 1024),))
    expert_ids_keys = jax.random.split(jax.random.fold_in(arg_keys[2], 1), TOKENS // TOK_DEV)
    expert_ids_turns = jax.random.permutation(jax.random.fold_in(arg_keys[2], 3), TOKENS // TOK_DEV)
    expert_ids = jax.vmap(lambda own, number: routed_block(jax.random.fold_in(arg_keys[2], 2), own, number, TOK_DEV, EXPERTS, TOP, CAP, 2))(expert_ids_keys, expert_ids_turns).reshape((TOKENS, TOP))
    gates = jnp.clip(0.25 + 0.75 * jax.random.uniform(arg_keys[3], (TOKENS, TOP), jnp.float32) ** block_levels(arg_keys[3], (TOKENS, TOP), ((0, 1024),), -0.2, 0.2), 0.25, 1.0).astype(jnp.bfloat16)
    gate_proj = normal_values(arg_keys[4], (EXPERTS, FF, D), D ** -0.5, 0.09375, ((0, 8), (1, 8)))
    up_proj = normal_values(arg_keys[5], (EXPERTS, FF, D), D ** -0.5, 0.09375, ((0, 8), (1, 8)))
    down_proj = normal_values(arg_keys[6], (EXPERTS, FF, D), FF ** -0.5, 0.15625, ((0, 8), (1, 8)))
    return {"tokens": tokens, "out_grad": out_grad, "expert_ids": expert_ids, "gates": gates, "gate_proj": gate_proj, "up_proj": up_proj, "down_proj": down_proj}


def reference(tokens, out_grad, expert_ids, gates, gate_proj, up_proj, down_proj):
    block_rows = TOKENS // N_DP
    ff_shard = FF // N_TP
    token_blocks = tokens.reshape(N_DP, block_rows, D)
    grad_blocks = out_grad.reshape(N_DP, block_rows, D)
    id_blocks = expert_ids.reshape(N_DP, block_rows, TOP)
    weight_blocks = gates.reshape(N_DP, block_rows, TOP)
    grad_scale = 1.0 / math.sqrt(TOKENS)

    def per_expert(total, expert):
        gate_w = gate_proj[expert]
        up_w = up_proj[expert]
        down_w = down_proj[expert]

        def per_block(sums, inputs):
            block_tokens, block_grads, block_ids, block_gates = inputs
            chosen = block_ids == expert
            coefficient = lax.optimization_barrier(jnp.sum(jnp.where(chosen, block_gates.astype(jnp.float32), jnp.float32(0.0)), axis=1))
            routed = jnp.any(chosen, axis=1)
            scaled = (coefficient[:, None] * block_grads.astype(jnp.float32)).astype(jnp.bfloat16)
            pre_gate = jnp.dot(block_tokens, gate_w.T, preferred_element_type=jnp.float32)
            pre_up = jnp.dot(block_tokens, up_w.T, preferred_element_type=jnp.float32)
            sigmoid_part = jax.nn.sigmoid(pre_gate)
            activated = pre_gate * sigmoid_part
            hidden = (activated * pre_up).astype(jnp.bfloat16)
            d_hidden = jnp.dot(scaled, down_w.T, preferred_element_type=jnp.float32)
            d_up = (d_hidden * activated).astype(jnp.bfloat16)
            d_gate = (d_hidden * pre_up * sigmoid_part * (1.0 + pre_gate * (1.0 - sigmoid_part))).astype(jnp.bfloat16)
            shares = jnp.einsum('ntf,tfd->ntd', d_gate.reshape(block_rows, N_TP, ff_shard).astype(jnp.float32), gate_w.reshape(N_TP, ff_shard, D).astype(jnp.float32))
            shares = shares + jnp.einsum('ntf,tfd->ntd', d_up.reshape(block_rows, N_TP, ff_shard).astype(jnp.float32), up_w.reshape(N_TP, ff_shard, D).astype(jnp.float32))
            shares = lax.optimization_barrier(shares.astype(jnp.bfloat16)).astype(jnp.float32)
            expert_grad = lax.optimization_barrier(jnp.sum(shares, axis=1)).astype(jnp.bfloat16)
            picked = jnp.where(routed[:, None], expert_grad.astype(jnp.float32), jnp.float32(0.0))
            part_gate = jnp.dot(d_gate.T, block_tokens, preferred_element_type=jnp.float32)
            part_up = jnp.dot(d_up.T, block_tokens, preferred_element_type=jnp.float32)
            part_down = jnp.dot(hidden.T, scaled, preferred_element_type=jnp.float32)
            parts = lax.optimization_barrier((part_gate.astype(jnp.bfloat16), part_up.astype(jnp.bfloat16), part_down.astype(jnp.bfloat16)))
            sums = (sums[0] + parts[0].astype(jnp.float32), sums[1] + parts[1].astype(jnp.float32), sums[2] + parts[2].astype(jnp.float32))
            return (sums, picked)
        start = (jnp.zeros((FF, D), jnp.float32), jnp.zeros((FF, D), jnp.float32), jnp.zeros((FF, D), jnp.float32))
        sums, picked = lax.scan(per_block, start, (token_blocks, grad_blocks, id_blocks, weight_blocks))
        return (total + picked, (sums[0] * grad_scale, sums[1] * grad_scale, sums[2] * grad_scale))
    total = jnp.zeros((N_DP, block_rows, D), jnp.float32)
    total, grads = lax.scan(per_expert, total, jnp.arange(EXPERTS, dtype=jnp.int32))
    token_grad = total.reshape(TOKENS, D).astype(jnp.bfloat16)
    return (token_grad, grads[0], grads[1], grads[2])
```

```python
import functools
import math

import jax
import jax.numpy as jnp
from jax import lax
from jax.experimental import pallas as pl
from jax.experimental.pallas import tpu as pltpu
from jax.sharding import PartitionSpec as P

BF = jnp.bfloat16
F32 = jnp.float32
CHIPS = 4
CTX = 8
TOK = 4
CAP = 2
ROWS = 16


def dot(a, b):
    return jnp.dot(a, b, preferred_element_type=F32)


def dot_t(a, b):
    return lax.dot_general(a, b, (((1,), (1,)), ((), ())), preferred_element_type=F32)


def iota(shape, dim):
    return lax.broadcasted_iota(jnp.int32, shape, dim)


class Copies:
    def __init__(self, send_sems, recv_sems):
        self.send_sems, self.recv_sems = send_sems, recv_sems
        self.used = 0
        self.sent = []

    def take(self, count=1):
        self.used += count
        return self.used - count

    def make(self, src, dst, sem, device):
        return pltpu.make_async_remote_copy(
            src_ref=src,
            dst_ref=dst,
            send_sem=self.send_sems.at[sem],
            recv_sem=self.recv_sems.at[sem],
            device_id=device,
            device_id_type=pl.DeviceIdType.MESH,
        )

    def send(self, src, dst, sem, device):
        copy = self.make(src, dst, sem, device)
        copy.start()
        self.sent.append(copy)

    def arrived(self, ref, sem, device):
        self.make(ref, ref, sem, device).wait_recv()

    def drain(self):
        for copy in self.sent:
            copy.wait_send()
        self.sent = []


class PlaneGather:
    def __init__(self, copies, n_tp, ref_a, ref_b, split_b):
        self.c, self.n = copies, n_tp
        self.half = n_tp // 2
        self.a, self.b, self.split_b = ref_a, ref_b, split_b
        self.ctx, self.t = lax.axis_index("ctx"), lax.axis_index("tp")
        self.x, self.k = self.ctx // 2, self.ctx % 2
        take = copies.take
        self.sem_a1 = [take() for _ in range(CHIPS)]
        self.sem_a = {(s, d): take() for s in range(1, self.half + 1) for d in (1, -1)}
        self.sem_b = {(s, d): take() for s in range(1, self.half + 1) for d in (1, -1)}
        self.sem_x = {(o, d): take() for o in self.offsets() for d in (1, -1)}
        self.sem_f = {o: take() for o in self.offsets()}
        self.sem_sa = {o: take() for o in self.offsets()}
        self.sem_sb = {o: take() for o in self.offsets()}

    def offsets(self):
        return list(range(-(self.half - 1), self.half + 1))

    def row(self, o):
        return (self.t + o + self.n) % self.n

    def chip(self, d):
        return (self.x + d + CHIPS) % CHIPS

    def at_chip(self, d):
        return {"ctx": 2 * self.chip(d) + self.k}

    def at_row(self, d):
        return {"tp": self.row(d)}

    def sibling(self):
        return {"ctx": 2 * self.x + 1 - self.k}

    def block(self, o, d):
        return self.row(o) * CTX + self.k * CHIPS + self.chip(d)

    def four(self, o, core):
        return self.row(o) * CTX + core * CHIPS

    def pass_a(self, o, s, d):
        if s < self.half:
            ref = self.a(self.four(o, self.k), 4)
        else:
            ref = self.a(self.four(o, self.k) + (0 if d > 0 else 2), 2)
        self.c.send(ref, ref, self.sem_a[s, d], self.at_row(d))

    def wait_a(self, o, s, d):
        if s < self.half:
            ref = self.a(self.four(o, self.k), 4)
        else:
            ref = self.a(self.four(o, self.k) + (0 if d > 0 else 2), 2)
        self.c.arrived(ref, self.sem_a[s, d], self.at_row(-d))

    def part_b(self, o, s, d):
        blk = self.block(o, 0)
        return self.b(blk, 1) if s < self.half else self.split_b(blk, 0 if d > 0 else 1)

    def pass_b(self, o, s, d):
        ref = self.part_b(o, s, d)
        self.c.send(ref, ref, self.sem_b[s, d], self.at_row(d))

    def wait_b(self, o, s, d):
        self.c.arrived(self.part_b(o, s, d), self.sem_b[s, d], self.at_row(-d))

    def along_x(self, o):
        ref = self.b(self.block(o, 0), 1)
        for d in (1, -1):
            self.c.send(ref, ref, self.sem_x[o, d], self.at_chip(d))

    def turn(self, o):
        return 1 if o <= 0 else -1

    def onward_x(self, o):
        for d in (1, -1):
            self.c.arrived(self.b(self.block(o, -d), 1), self.sem_x[o, d], self.at_chip(-d))
        d = self.turn(o)
        ref = self.b(self.block(o, -d), 1)
        self.c.send(ref, ref, self.sem_f[o], self.at_chip(d))

    def to_sibling_a(self, o):
        ref = self.a(self.four(o, self.k), 4)
        self.c.send(ref, ref, self.sem_sa[o], self.sibling())

    def to_sibling_b(self, o):
        d = self.turn(o)
        self.c.arrived(self.b(self.block(o, 2), 1), self.sem_f[o], self.at_chip(-d))
        ref = self.b(self.four(o, self.k), 4)
        self.c.send(ref, ref, self.sem_sb[o], self.sibling())

    def begin(self):
        own = self.a(self.block(0, 0), 1)
        for d in range(1, CHIPS):
            self.c.send(own, own, self.sem_a1[d], self.at_chip(d))
        self.pass_b(0, 1, 1)
        self.pass_b(0, 1, -1)
        self.along_x(0)

    def rows_begin(self):
        for d in range(1, CHIPS):
            self.c.arrived(self.a(self.block(0, -d), 1), self.sem_a1[d], self.at_chip(-d))
        self.pass_a(0, 1, 1)
        self.pass_a(0, 1, -1)
        self.to_sibling_a(0)

    def at_step(self, s):
        return [-s, s] if s < self.half else [self.half]

    def step(self, s):
        last = s == self.half
        self.wait_b(self.half if last else -s, s, 1)
        self.wait_b(self.half if last else s, s, -1)
        if not last:
            self.pass_b(-s, s + 1, 1)
            self.pass_b(s, s + 1, -1)
        for o in self.at_step(s):
            self.along_x(o)
        self.wait_a(self.half if last else -s, s, 1)
        self.wait_a(self.half if last else s, s, -1)
        if not last:
            self.pass_a(-s, s + 1, 1)
            self.pass_a(s, s + 1, -1)
        for o in self.at_step(s):
            self.to_sibling_a(o)
        before = [0] if s == 1 else self.at_step(s - 1)
        for o in before:
            self.onward_x(o)
        if s > 1:
            for o in [0] if s == 2 else self.at_step(s - 2):
                self.to_sibling_b(o)

    def finish(self):
        for o in self.at_step(self.half):
            self.onward_x(o)
        if self.half > 1:
            for o in self.at_step(self.half - 1):
                self.to_sibling_b(o)
        else:
            self.to_sibling_b(0)
        for o in self.at_step(self.half):
            self.to_sibling_b(o)

    def from_sibling(self):
        for o in self.offsets():
            self.c.arrived(self.a(self.four(o, 1 - self.k), 4), self.sem_sa[o], self.sibling())
            self.c.arrived(self.b(self.four(o, 1 - self.k), 4), self.sem_sb[o], self.sibling())


def kernel(
    sizes, xd_ref, ids_ref, gates_ref, gate_hbm, up_hbm, down_hbm,
    tok_ref, gate_ref, up_ref, down_ref,
    ga, gb, g2, zp, wgu, wd, rx, rd, hb, xc, acc, part, rs_in, rs_out, xs, xr,
    send_sems, recv_sems, load_sems,
):
    n_dp, n_tp, width, units, scale = sizes
    quarter = width // 4
    half_z, half_t = n_dp // 2, n_tp // 2
    z, ctx, t = lax.axis_index("dp"), lax.axis_index("ctx"), lax.axis_index("tp")
    place = (ctx % 2) * CHIPS + ctx // 2
    me = t * CTX + place

    barrier = pltpu.get_barrier_semaphore()
    for d in range(1, n_dp):
        pl.semaphore_signal(
            barrier, inc=1, device_id={"dp": (z + d) % n_dp}, device_id_type=pl.DeviceIdType.MESH
        )
    for d in range(1, CTX):
        pl.semaphore_signal(
            barrier, inc=1, device_id={"ctx": (ctx + d) % CTX}, device_id_type=pl.DeviceIdType.MESH
        )
    rows = (1, -1) if n_tp > 2 else (1,)
    for d in rows:
        pl.semaphore_signal(
            barrier,
            inc=1,
            device_id={"tp": (t + d + n_tp) % n_tp},
            device_id_type=pl.DeviceIdType.MESH,
        )
    loads = [
        pltpu.make_async_copy(gate_hbm, wgu.at[pl.ds(0, units)], load_sems.at[0]),
        pltpu.make_async_copy(up_hbm, wgu.at[pl.ds(units, units)], load_sems.at[1]),
        pltpu.make_async_copy(down_hbm, wd, load_sems.at[2]),
    ]
    for load in loads:
        load.start()

    ga[me, :, 0:quarter] = jnp.concatenate(
        [xd_ref[:, 0:quarter], xd_ref[:, quarter : 2 * quarter]], axis=0
    ).astype(BF)
    gb[me] = jnp.concatenate(
        [xd_ref[:, 2 * quarter : 3 * quarter], xd_ref[:, 3 * quarter :]], axis=0
    ).astype(BF)
    for i in range(n_dp):
        zp[i] = jnp.concatenate(
            [xd_ref[:, 256 * i : 256 * i + 128], xd_ref[:, 256 * i + 128 : 256 * i + 256]], axis=0
        ).astype(BF)
    g2[me, z] = zp[z]
    line, lane = iota((ROWS, 128), 0), iota((ROWS, 128), 1)
    expert = line % 8
    inner = lane % ROWS
    first = ((inner // 4) * 16 + 2 * place + 1).astype(F32)
    is_grad = (inner // 4) % 2 == 1
    count = jnp.zeros((ROWS, 128), F32)
    meta = jnp.zeros((ROWS, 128), F32)
    for n in range(TOK):
        coefficient = jnp.where(expert == ids_ref[n, 0], gates_ref[n, 0], 0.0) + jnp.where(
            expert == ids_ref[n, 1], gates_ref[n, 1], 0.0
        )
        named = (expert == ids_ref[n, 0]) | (expert == ids_ref[n, 1])
        factor = jnp.where(is_grad, coefficient, 1.0)
        value = jnp.where(line < 8, first + count, factor)
        meta = jnp.where(named & (inner % 4 == n) & (lane // ROWS == place), value, meta)
        count = count + jnp.where(named, 1.0, 0.0)
    ga[me, :, quarter:] = meta.astype(BF)

    pl.semaphore_wait(barrier, n_dp - 1 + CTX - 1 + len(rows))

    copies = Copies(send_sems, recv_sems)
    plane1 = PlaneGather(
        copies,
        n_tp,
        lambda at, size: ga.at[pl.ds(at, size)],
        lambda at, size: gb.at[pl.ds(at, size)],
        lambda at, part: gb.at[pl.ds(at, 1), :, pl.ds(part * (quarter // 2), quarter // 2)],
    )
    low, quart = n_dp // 2, n_dp // 4
    plane2 = PlaneGather(
        copies,
        n_tp,
        lambda at, size: g2.at[pl.ds(at, size), pl.ds(0, low)],
        lambda at, size: g2.at[pl.ds(at, size), pl.ds(low, low)],
        lambda at, part: g2.at[pl.ds(at, 1), pl.ds(low + part * quart, quart)],
    )
    sem_z = copies.take(n_dp)
    plane1.begin()
    for d in range(1, n_dp):
        to = (z + d) % n_dp
        copies.send(zp.at[to], g2.at[me, z], sem_z + d, {"dp": to})
    plane1.rows_begin()
    for s in range(1, half_t + 1):
        plane1.step(s)
    plane1.finish()
    for d in range(1, n_dp):
        source = (z - d + n_dp) % n_dp
        copies.arrived(g2.at[me, source], sem_z + d, {"dp": source})
    plane2.begin()
    plane1.from_sibling()
    for load in loads:
        load.wait()

    table = jnp.zeros((ROWS, 128), F32)
    for r in range(n_tp):
        total = ga[r * CTX, :, quarter:].astype(F32)
        for i in range(1, CTX):
            total = total + ga[r * CTX + i, :, quarter:].astype(F32)
        slot = jnp.sum(jnp.where(line == ctx, total, 0.0), axis=0, keepdims=True)
        factor = jnp.sum(jnp.where(line == 8 + ctx, total, 0.0), axis=0, keepdims=True)
        table = table + jnp.where(line == r, slot, 0.0) + jnp.where(line == 8 + r, factor, 0.0)
    hb[z, 3 * units :, :] = table.astype(BF)

    def choosing(tab, r):
        want = tab[r : r + 1, :]
        value = tab[8 + r : 9 + r, :]
        number = (iota((64, 128), 0) + 1).astype(F32)
        return jnp.where(number == want, value, 0.0).astype(BF)

    if n_tp * CTX * CAP < 128:
        rx[...] = jnp.zeros_like(rx)
        rd[...] = jnp.zeros_like(rd)
    for r in range(n_tp):
        pick = choosing(table, r)
        for side, block in enumerate((ga, gb)):
            got = dot(pick, block[r * CTX : (r + 1) * CTX, :, 0:quarter].reshape(128, quarter))
            got = got.astype(BF)
            for h in range(2):
                at = (2 * side + h) * quarter
                rx[16 * r : 16 * r + 16, at : at + quarter] = got[32 * h : 32 * h + 16]
                rd[16 * r : 16 * r + 16, at : at + quarter] = got[32 * h + 16 : 32 * h + 32]
    both = dot_t(wgu[:, 0:quarter], rx[:, 0:quarter])
    d_hidden = dot_t(wd[:, 0:quarter], rd[:, 0:quarter])
    for j in range(1, 4):
        cols = slice(j * quarter, (j + 1) * quarter)
        both = both + dot_t(wgu[:, cols], rx[:, cols])
        d_hidden = d_hidden + dot_t(wd[:, cols], rd[:, cols])
    pre_gate, pre_up = both[:units], both[units:]
    sigmoid = 1.0 / (1.0 + jnp.exp(-pre_gate))
    activated = pre_gate * sigmoid
    d_up = d_hidden * activated
    d_gate = d_hidden * pre_up * (sigmoid * (1.0 + pre_gate * (1.0 - sigmoid)))
    hb[z, 0:units, :] = d_gate.astype(BF)
    hb[z, units : 2 * units, :] = d_up.astype(BF)
    hb[z, 2 * units : 3 * units, :] = (activated * pre_up).astype(BF)

    sem_ring = {(s, d): copies.take() for s in range(1, half_z + 1) for d in (1, -1)}
    lines = 3 * units + ROWS
    cut = (lines // 2 + 15) // 16 * 16

    def ring_part(o, s, d):
        b = (z + o + n_dp) % n_dp
        if s < half_z:
            return hb.at[b]
        return hb.at[b, pl.ds(0, cut)] if d > 0 else hb.at[b, pl.ds(cut, lines - cut)]

    def ring_send(o, s, d):
        ref = ring_part(o, s, d)
        copies.send(ref, ref, sem_ring[s, d], {"dp": (z + d + n_dp) % n_dp})

    def ring_wait(o, s, d):
        copies.arrived(ring_part(o, s, d), sem_ring[s, d], {"dp": (z - d + n_dp) % n_dp})

    ring_send(0, 1, 1)
    ring_send(0, 1, -1)

    by_slot = jnp.concatenate([d_gate, d_up], axis=0).T.astype(BF)
    step_cols = min(512, width)

    @pl.loop(0, width // step_cols)
    def _(i):
        cols = pl.ds(pl.multiple_of(i * step_cols, step_cols), step_cols)
        part[:, cols] = dot(by_slot, wgu[:, cols])

    sem_rs = {(s, d): copies.take() for s in range(1, half_t + 1) for d in (1, -1)}

    def share(o):
        u = (t + o + n_tp) % n_tp
        return part[pl.ds(pl.multiple_of(u * 16, 16), 16), :]

    def rs_slot(s, d):
        return s - 1 if d > 0 else half_t + s - 1

    def rs_send(s, d):
        total = share(half_t - s + 1 if d > 0 else s - half_t)
        if s > 1:
            total = total + rs_in[rs_slot(s - 1, d)].astype(F32)
        rs_out[rs_slot(s, d)] = total.astype(BF)
        copies.send(
            rs_out.at[rs_slot(s, d)],
            rs_in.at[rs_slot(s, d)],
            sem_rs[s, d],
            {"tp": (t + d + n_tp) % n_tp},
        )

    def rs_wait(s, d):
        copies.arrived(rs_in.at[rs_slot(s, d)], sem_rs[s, d], {"tp": (t - d + n_tp) % n_tp})

    def rs_step(s):
        if s > 1:
            rs_wait(s - 1, 1)
            if s - 1 < half_t:
                rs_wait(s - 1, -1) if s - 1 <= half_t - 1 else None
        if s <= half_t:
            rs_send(s, 1)
        if s <= half_t - 1:
            rs_send(s, -1)

    sem_ctx = copies.take(CTX)

    def to_tokens():
        total = share(0) + rs_in[rs_slot(half_t, 1)].astype(F32)
        if half_t > 1:
            total = total + rs_in[rs_slot(half_t - 1, -1)].astype(F32)
        total = total.astype(BF)
        stacked = jnp.concatenate([total[:, j * quarter : (j + 1) * quarter] for j in range(4)], 0)
        want = jnp.sum(jnp.where(line == t, table, 0.0), axis=0, keepdims=True)
        want = jnp.broadcast_to(want, (128, 128)).T[:, 0:64]
        pick = jnp.where((iota((128, 64), 1) + 1).astype(F32) == want, 1.0, 0.0).astype(BF)
        spread = dot(pick, stacked).astype(BF)
        for i in range(CTX):
            xs[i] = spread[16 * i : 16 * i + 16]
        for d in range(1, CTX):
            to = (ctx + d) % CTX
            copies.send(
                xs.at[(to % 2) * CHIPS + to // 2], xr.at[ctx], sem_ctx + d, {"ctx": to}
            )

    def tokens_out():
        total = xs[place].astype(F32)
        for d in range(1, CTX):
            source = (ctx - d + CTX) % CTX
            copies.arrived(xr.at[source], sem_ctx + d, {"ctx": source})
        for d in range(1, CTX):
            total = total + xr[(ctx - d + CTX) % CTX].astype(F32)
        for j in range(4):
            tok_ref[:, j * quarter : (j + 1) * quarter] = total[4 * j : 4 * j + 4].astype(BF)

    acc[...] = jnp.zeros_like(acc)
    if n_tp * CTX * CAP < 128:
        xc[...] = jnp.zeros_like(xc)

    def replica(o):
        b = (z + o + n_dp) % n_dp
        tab = hb[b, 3 * units :, :].astype(F32)
        for r in range(n_tp):
            got = dot(choosing(tab, r), g2[r * CTX : (r + 1) * CTX, b].reshape(128, 128))
            got = got.astype(BF)
            for h in range(2):
                for q in range(2):
                    at = (2 * h + q) * 16
                    xc[q, 16 * r : 16 * r + 16, 128 * h : 128 * h + 128] = got[at : at + 16]
        acc[0 : 2 * units, :] += dot(hb[b, 0 : 2 * units, :], xc[0])
        acc[2 * units :, :] += dot(hb[b, 2 * units : 3 * units, :], xc[1])

    def replicas(start, count, stride=1):
        lax.fori_loop(0, count, lambda i, _: (replica(start + i * stride), 0)[1], 0)

    todo = [plane2.rows_begin]
    todo += [functools.partial(plane2.step, s) for s in range(1, half_t + 1)]
    todo += [plane2.finish, plane2.from_sibling]
    grads = [functools.partial(rs_step, s) for s in range(1, half_t + 2)]
    grads += [to_tokens, tokens_out]
    done = None
    for s in range(1, half_z + 1):
        last = s == half_z
        if grads:
            grads.pop(0)()
        if todo:
            todo.pop(0)()
        ring_wait(half_z if last else -s, s, 1)
        ring_wait(half_z if last else s, s, -1)
        if not last:
            ring_send(-s, s + 1, 1)
            ring_send(s, s + 1, -1)
        if last:
            while todo:
                todo.pop(0)()
            while grads:
                grads.pop(0)()
        if not todo:
            if done is None:
                replicas(-s if not last else 1 - s, 2 * s + 1 if not last else 2 * s)
            elif not last:
                replicas(-s, 2, 2 * s)
            else:
                replicas(s, 1)
            done = s
    gate_ref[...] = acc[0:units, :] * scale
    up_ref[...] = acc[units : 2 * units, :] * scale
    down_ref[...] = acc[2 * units :, :] * scale
    copies.drain()


def sem_count(n_dp, n_tp):
    plane = CHIPS + 4 * (n_tp // 2) + 5 * n_tp
    return 2 * plane + n_dp + 2 * (n_dp // 2) + 2 * (n_tp // 2) + CTX


def local(tokens, out_grad, expert_ids, gates, gate_proj, up_proj, down_proj):
    n_dp, n_tp = lax.axis_size("dp"), lax.axis_size("tp")
    width, units = tokens.shape[1], gate_proj.shape[1]
    quarter = width // 4
    devices = n_tp * CTX
    scale = 1.0 / math.sqrt(tokens.shape[0] * n_dp * devices)
    xd = jnp.concatenate([tokens, out_grad], axis=0).astype(F32)
    vmem = pl.BlockSpec(memory_space=pltpu.VMEM)
    smem = pl.BlockSpec(memory_space=pltpu.SMEM)
    hbm = pl.BlockSpec(memory_space=pl.ANY)
    grad = jax.ShapeDtypeStruct((units, width // n_dp), F32)
    sems = sem_count(n_dp, n_tp)
    token_grad, gate_grad, up_grad, down_grad = pl.pallas_call(
        functools.partial(kernel, (n_dp, n_tp, width, units, scale)),
        out_shape=(jax.ShapeDtypeStruct(tokens.shape, BF), grad, grad, grad),
        in_specs=[vmem, smem, smem, hbm, hbm, hbm],
        out_specs=(vmem, vmem, vmem, vmem),
        scratch_shapes=[
            pltpu.VMEM((devices, ROWS, quarter + 128), BF),
            pltpu.VMEM((devices, ROWS, quarter), BF),
            pltpu.VMEM((devices, n_dp, ROWS, 128), BF),
            pltpu.VMEM((n_dp, ROWS, 128), BF),
            pltpu.VMEM((2 * units, width), BF),
            pltpu.VMEM((units, width), BF),
            pltpu.VMEM((128, width), BF),
            pltpu.VMEM((128, width), BF),
            pltpu.VMEM((n_dp, 3 * units + ROWS, 128), BF),
            pltpu.VMEM((2, 128, 256), BF),
            pltpu.VMEM((3 * units, 256), F32),
            pltpu.VMEM((128, width), F32),
            pltpu.VMEM((n_tp, 16, width), BF),
            pltpu.VMEM((n_tp, 16, width), BF),
            pltpu.VMEM((CTX, ROWS, quarter), BF),
            pltpu.VMEM((CTX, ROWS, quarter), BF),
            pltpu.SemaphoreType.DMA((sems,)),
            pltpu.SemaphoreType.DMA((sems,)),
            pltpu.SemaphoreType.DMA((3,)),
        ],
        compiler_params=pltpu.CompilerParams(
            collective_id=0, has_side_effects=True, vmem_limit_bytes=48 * 2**20
        ),
    )(
        xd,
        expert_ids,
        gates.astype(F32),
        gate_proj[0],
        up_proj[0],
        down_proj[0],
    )
    return token_grad, gate_grad[None], up_grad[None], down_grad[None]


def solution(mesh):
    rows = P(("dp", "ctx", "tp"), None)
    weights = P("ctx", "tp", None)
    grads = P("ctx", "tp", "dp")
    return jax.shard_map(
        local,
        mesh=mesh,
        in_specs=(rows, rows, rows, rows, weights, weights, weights),
        out_specs=(rows, grads, grads, grads),
        check_vma=False,
    )
```

```python
import functools
import math

import jax
import jax.numpy as jnp
from jax import lax
from jax.experimental import pallas as pl
from jax.experimental.pallas import tpu as pltpu
from jax.sharding import PartitionSpec as P

BF = jnp.bfloat16
F32 = jnp.float32
CHIPS = 4
CTX = 8
TOK = 4
CAP = 2
PIECES = 4
RS_AT = 2
SPLIT = 2
ROWS = 16


def dot(a, b):
    return jnp.dot(a, b, preferred_element_type=F32)


def dot_t(a, b):
    return lax.dot_general(a, b, (((1,), (1,)), ((), ())), preferred_element_type=F32)


def iota(shape, dim):
    return lax.broadcasted_iota(jnp.int32, shape, dim)


class Copies:
    def __init__(self, send_sems, recv_sems):
        self.send_sems, self.recv_sems = send_sems, recv_sems
        self.used = 0
        self.sent = []

    def take(self, count=1):
        self.used += count
        return self.used - count

    def make(self, src, dst, sem, device):
        return pltpu.make_async_remote_copy(
            src_ref=src,
            dst_ref=dst,
            send_sem=self.send_sems.at[sem],
            recv_sem=self.recv_sems.at[sem],
            device_id=device,
            device_id_type=pl.DeviceIdType.MESH,
        )

    def send(self, src, dst, sem, device):
        copy = self.make(src, dst, sem, device)
        copy.start()
        self.sent.append(copy)

    def arrived(self, ref, sem, device):
        self.make(ref, ref, sem, device).wait_recv()

    def drain(self):
        for copy in self.sent:
            copy.wait_send()
        self.sent = []


class Plane:
    def __init__(self, copies, n_tp):
        self.c, self.n, self.half = copies, n_tp, n_tp // 2
        ctx, self.t = lax.axis_index("ctx"), lax.axis_index("tp")
        self.x, self.k = ctx // 2, ctx % 2
        self.sibling = {"ctx": 2 * self.x + 1 - self.k}

    def offsets(self):
        return list(range(-(self.half - 1), self.half + 1))

    def row(self, o):
        return (self.t + o + self.n) % self.n

    def chip(self, d):
        return (self.x + d + CHIPS) % CHIPS

    def at_chip(self, d):
        return {"ctx": 2 * self.chip(d) + self.k}

    def at_row(self, d):
        return {"tp": self.row(d)}

    def block(self, o, d):
        return self.row(o) * CTX + self.k * CHIPS + self.chip(d)

    def four(self, o, core):
        return self.row(o) * CTX + core * CHIPS

    def at_step(self, s):
        return [0] if s == 0 else [-s, s] if s < self.half else [self.half]


class ChipsFirst(Plane):
    def __init__(self, copies, n_tp, ref):
        super().__init__(copies, n_tp)
        self.ref = ref
        self.sem_x = [copies.take() for _ in range(CHIPS)]
        self.sem_y = {
            (s, d, e): copies.take()
            for s in range(1, self.half + 1)
            for d in (1, -1)
            for e in range(CHIPS)
            if self.goes(s, d, e)
        }
        self.sem_s = {o: copies.take() for o in self.offsets()}

    def goes(self, s, d, e):
        return s < self.half or (e < 2) == (d > 0)

    def send(self, o, s, d, e):
        if self.goes(s, d, e):
            ref = self.ref(self.block(o, -e), 1)
            self.c.send(ref, ref, self.sem_y[s, d, e], self.at_row(d))

    def wait(self, o, s, d, e):
        if self.goes(s, d, e):
            ref = self.ref(self.block(o, -e), 1)
            self.c.arrived(ref, self.sem_y[s, d, e], self.at_row(-d))

    def begin(self):
        own = self.ref(self.block(0, 0), 1)
        for d in (1, 3, 2):
            self.c.send(own, own, self.sem_x[d], self.at_chip(d))
        self.send(0, 1, 1, 0)
        self.send(0, 1, -1, 0)

    def rows_begin(self):
        for e in (1, 3, 2):
            self.c.arrived(self.ref(self.block(0, -e), 1), self.sem_x[e], self.at_chip(-e))
            self.send(0, 1, 1, e)
            self.send(0, 1, -1, e)
        self.to_sibling(0)

    def step(self, s):
        last = s == self.half
        for e in (0, 1, 3, 2):
            self.wait(self.half if last else -s, s, 1, e)
            if not last:
                self.send(-s, s + 1, 1, e)
            self.wait(self.half if last else s, s, -1, e)
            if not last:
                self.send(s, s + 1, -1, e)
        for o in self.at_step(s):
            self.to_sibling(o)

    def to_sibling(self, o):
        ref = self.ref(self.four(o, self.k), 4)
        self.c.send(ref, ref, self.sem_s[o], self.sibling)

    def from_sibling(self, o):
        self.c.arrived(self.ref(self.four(o, 1 - self.k), 4), self.sem_s[o], self.sibling)


class RowsFirst(Plane):
    def __init__(self, copies, n_tp, ref, split):
        super().__init__(copies, n_tp)
        self.ref, self.split = ref, split
        steps = range(1, self.half + 1)
        self.sem_y = {(s, d): copies.take() for s in steps for d in (1, -1)}
        self.sem_x = {(o, d): copies.take() for o in self.offsets() for d in (1, -1)}
        self.sem_f = {o: copies.take() for o in self.offsets()}
        self.sem_s = {o: copies.take() for o in self.offsets()}

    def part(self, o, s, d):
        at = self.block(o, 0)
        return self.ref(at, 1) if s < self.half else self.split(at, 0 if d > 0 else 1)

    def send(self, o, s, d):
        ref = self.part(o, s, d)
        self.c.send(ref, ref, self.sem_y[s, d], self.at_row(d))

    def wait(self, o, s, d):
        self.c.arrived(self.part(o, s, d), self.sem_y[s, d], self.at_row(-d))

    def begin(self):
        self.send(0, 1, 1)
        self.send(0, 1, -1)

    def step(self, s):
        last = s == self.half
        self.wait(self.half if last else -s, s, 1)
        if not last:
            self.send(-s, s + 1, 1)
        self.wait(self.half if last else s, s, -1)
        if not last:
            self.send(s, s + 1, -1)

    def along(self, s):
        for o in self.at_step(s):
            ref = self.ref(self.block(o, 0), 1)
            for d in (1, -1):
                self.c.send(ref, ref, self.sem_x[o, d], self.at_chip(d))

    def turn(self, o):
        return 1 if o <= 0 else -1

    def onward(self, s):
        for o in self.at_step(s):
            for d in (1, -1):
                self.c.arrived(self.ref(self.block(o, -d), 1), self.sem_x[o, d], self.at_chip(-d))
            d = self.turn(o)
            ref = self.ref(self.block(o, -d), 1)
            self.c.send(ref, ref, self.sem_f[o], self.at_chip(d))

    def to_sibling(self, s):
        for o in self.at_step(s):
            d = self.turn(o)
            self.c.arrived(self.ref(self.block(o, 2), 1), self.sem_f[o], self.at_chip(-d))
            ref = self.ref(self.four(o, self.k), 4)
            self.c.send(ref, ref, self.sem_s[o], self.sibling)

    def from_sibling(self, o):
        self.c.arrived(self.ref(self.four(o, 1 - self.k), 4), self.sem_s[o], self.sibling)


def kernel(
    sizes, xd_ref, gate_hbm, up_hbm, down_hbm,
    tok_ref, gate_ref, up_ref, down_ref,
    ga, gb, g2, zp, wgu, wd, rx, rd, hb, xc, acc, part, rs_in, rs_out, xs, xr,
    send_sems, recv_sems, load_sems,
):
    n_dp, n_tp, width, units, scale = sizes
    quarter = width // 4
    half_z, half_t = n_dp // 2, n_tp // 2
    z, ctx, t = lax.axis_index("dp"), lax.axis_index("ctx"), lax.axis_index("tp")
    place = (ctx % 2) * CHIPS + ctx // 2
    me = t * CTX + place

    barrier = pltpu.get_barrier_semaphore()
    for d in range(1, n_dp):
        pl.semaphore_signal(
            barrier, inc=1, device_id={"dp": (z + d) % n_dp}, device_id_type=pl.DeviceIdType.MESH
        )
    for d in range(1, CTX):
        pl.semaphore_signal(
            barrier, inc=1, device_id={"ctx": (ctx + d) % CTX}, device_id_type=pl.DeviceIdType.MESH
        )
    rows = (1, -1) if n_tp > 2 else (1,)
    for d in rows:
        pl.semaphore_signal(
            barrier,
            inc=1,
            device_id={"tp": (t + d + n_tp) % n_tp},
            device_id_type=pl.DeviceIdType.MESH,
        )
    loads = [
        pltpu.make_async_copy(gate_hbm, wgu.at[pl.ds(0, units)], load_sems.at[0]),
        pltpu.make_async_copy(up_hbm, wgu.at[pl.ds(units, units)], load_sems.at[1]),
        pltpu.make_async_copy(down_hbm, wd, load_sems.at[2]),
    ]
    for load in loads:
        load.start()

    def stacked_rows(first, size):
        halves = [xd_ref[0:8, at : at + size] for at in (first, first + size)]
        return jnp.concatenate(halves, axis=0).astype(BF)

    ga[me, :, 0:quarter] = stacked_rows(0, quarter)
    gb[me] = stacked_rows(2 * quarter, quarter)
    for i in range(n_dp):
        zp[i] = stacked_rows(256 * i, 128)
    g2[me, z] = zp[z]
    line, lane = iota((ROWS, 128), 0), iota((ROWS, 128), 1)
    expert = (line % 8).astype(F32)
    inner = lane % ROWS
    first = ((inner // 4) * 16 + 2 * place + 1).astype(F32)
    is_grad = (inner // 4) % 2 == 1
    count = jnp.zeros((ROWS, 128), F32)
    meta = jnp.zeros((ROWS, 128), F32)
    routing = xd_ref[8:16, 0:128]
    for n in range(TOK):
        named, coefficient = line < 0, jnp.zeros((ROWS, 128), F32)
        for k in range(2):
            chosen = expert == routing[k : k + 1, n : n + 1]
            named = named | chosen
            coefficient = jnp.where(chosen, routing[k + 2 : k + 3, n : n + 1], coefficient)
        factor = jnp.where(is_grad, coefficient, 1.0)
        value = jnp.where(line < 8, first + count, factor)
        meta = jnp.where(named & (inner % 4 == n) & (lane // ROWS == place), value, meta)
        count = count + jnp.where(named, 1.0, 0.0)
    ga[me, :, quarter:] = meta.astype(BF)

    pl.semaphore_wait(barrier, n_dp - 1 + CTX - 1 + len(rows))

    copies = Copies(send_sems, recv_sems)
    a1 = ChipsFirst(copies, n_tp, lambda at, size: ga.at[pl.ds(at, size)])
    b1 = RowsFirst(
        copies,
        n_tp,
        lambda at, size: gb.at[pl.ds(at, size)],
        lambda at, part: gb.at[pl.ds(at, 1), :, pl.ds(part * (quarter // 2), quarter // 2)],
    )
    low = n_dp // 2
    a2 = ChipsFirst(copies, n_tp, lambda at, size: g2.at[pl.ds(at, size), pl.ds(0, low)])
    b2 = RowsFirst(
        copies,
        n_tp,
        lambda at, size: g2.at[pl.ds(at, size), pl.ds(low, low)],
        lambda at, part: g2.at[pl.ds(at, 1), pl.ds(low + part * (low // 2), low // 2)],
    )
    sem_z = copies.take(n_dp)

    def columns_send():
        for d in range(1, n_dp):
            to = (z + d) % n_dp
            copies.send(zp.at[to], g2.at[me, z], sem_z + d, {"dp": to})

    def columns_begin():
        for d in range(1, n_dp):
            source = (z - d + n_dp) % n_dp
            copies.arrived(g2.at[me, source], sem_z + d, {"dp": source})
        b2.begin()
        b2.along(0)
        a2.begin()

    begin_at = min(2, half_t)
    b1.begin()
    a1.begin()
    b1.along(0)
    columns_send()
    b1.step(1)
    b1.along(1)
    a1.rows_begin()
    b2_steps = 0
    for s in range(1, half_t + 1):
        if s < half_t:
            b1.step(s + 1)
            b1.along(s + 1)
        b1.onward(s - 1)
        if s == half_t:
            b1.onward(s)
        if s > 1:
            b1.to_sibling(s - 2)
        if s == begin_at:
            columns_begin()
        elif s > begin_at:
            b2_steps += 1
            b2.step(b2_steps)
            b2.along(b2_steps)
        a1.step(s)
    b1.to_sibling(half_t - 1)
    b1.to_sibling(half_t)
    if b2_steps + 1 < half_t:
        b2_steps += 1
        b2.step(b2_steps)
        b2.along(b2_steps)
    a2.rows_begin()
    for o in a1.offsets():
        a1.from_sibling(o)
        b1.from_sibling(o)
    for load in loads:
        load.wait()

    table = jnp.zeros((ROWS, 128), F32)
    for r in range(n_tp):
        total = ga[r * CTX, :, quarter:].astype(F32)
        for i in range(1, CTX):
            total = total + ga[r * CTX + i, :, quarter:].astype(F32)
        slot = jnp.sum(jnp.where(line == ctx, total, 0.0), axis=0, keepdims=True)
        factor = jnp.sum(jnp.where(line == 8 + ctx, total, 0.0), axis=0, keepdims=True)
        table = table + jnp.where(line == r, slot, 0.0) + jnp.where(line == 8 + r, factor, 0.0)
    hb[z, 3 * units :, :] = table.astype(BF)

    def choosing(tab, r):
        want = tab[r : r + 1, :]
        value = tab[8 + r : 9 + r, :]
        number = (iota((64, 128), 0) + 1).astype(F32)
        return jnp.where(number == want, value, 0.0).astype(BF)

    if n_tp * CTX * CAP < 128:
        rx[...] = jnp.zeros_like(rx)
        rd[...] = jnp.zeros_like(rd)
    for r in range(n_tp):
        pick = choosing(table, r)
        for side, block in enumerate((ga, gb)):
            got = dot(pick, block[r * CTX : (r + 1) * CTX, :, 0:quarter].reshape(128, quarter))
            got = got.astype(BF)
            for h in range(2):
                at = (2 * side + h) * quarter
                rx[16 * r : 16 * r + 16, at : at + quarter] = got[32 * h : 32 * h + 16]
                rd[16 * r : 16 * r + 16, at : at + quarter] = got[32 * h + 16 : 32 * h + 32]
    both = dot_t(wgu[:, 0:quarter], rx[:, 0:quarter])
    d_hidden = dot_t(wd[:, 0:quarter], rd[:, 0:quarter])
    for j in range(1, 4):
        cols = slice(j * quarter, (j + 1) * quarter)
        both = both + dot_t(wgu[:, cols], rx[:, cols])
        d_hidden = d_hidden + dot_t(wd[:, cols], rd[:, cols])
    pre_gate, pre_up = both[:units], both[units:]
    sigmoid = 1.0 / (1.0 + jnp.exp(-pre_gate))
    activated = pre_gate * sigmoid
    d_up = d_hidden * activated
    d_gate = d_hidden * pre_up * (sigmoid * (1.0 + pre_gate * (1.0 - sigmoid)))
    hb[z, 0:units, :] = d_gate.astype(BF)
    hb[z, units : 2 * units, :] = d_up.astype(BF)
    hb[z, 2 * units : 3 * units, :] = (activated * pre_up).astype(BF)

    lines = 3 * units + ROWS
    cuts = [lines * c // (16 * PIECES) * 16 for c in range(PIECES + 1)]
    pieces = range(PIECES)

    def ring_goes(s, d, c):
        return s < half_z or (c < PIECES // 2) == (d > 0)

    sem_ring = {
        (s, d, c): copies.take()
        for s in range(1, half_z + 1)
        for d in (1, -1)
        for c in pieces
        if ring_goes(s, d, c)
    }

    def ring_part(o, c):
        return hb.at[(z + o + n_dp) % n_dp, pl.ds(cuts[c], cuts[c + 1] - cuts[c])]

    def ring_send(o, s, d, c):
        if ring_goes(s, d, c):
            ref = ring_part(o, c)
            copies.send(ref, ref, sem_ring[s, d, c], {"dp": (z + d + n_dp) % n_dp})

    def ring_wait(o, s, d, c):
        if ring_goes(s, d, c):
            copies.arrived(ring_part(o, c), sem_ring[s, d, c], {"dp": (z - d + n_dp) % n_dp})

    for c in pieces:
        ring_send(0, 1, 1, c)
        ring_send(0, 1, -1, c)

    by_slot = jnp.concatenate([d_gate, d_up], axis=0).T.astype(BF)
    step_cols = min(512, width)

    @pl.loop(0, width // step_cols)
    def _(i):
        cols = pl.ds(pl.multiple_of(i * step_cols, step_cols), step_cols)
        part[:, cols] = dot(by_slot, wgu[:, cols])

    wide = width // SPLIT
    sem_rs = {
        (s, d, c): copies.take() for s in range(1, half_t + 1) for d in (1, -1) for c in range(SPLIT)
    }

    def share(o, c):
        at = pl.multiple_of((t + o + n_tp) % n_tp * 16, 16)
        return part[pl.ds(at, 16), c * wide : (c + 1) * wide]

    def rs_slot(s, d, c):
        return (s - 1 if d > 0 else half_t + s - 1) * SPLIT + c

    def rs_wait(s, d, c):
        ref = rs_in.at[rs_slot(s, d, c)]
        copies.arrived(ref, sem_rs[s, d, c], {"tp": (t - d + n_tp) % n_tp})

    def rs_send(s, d, c):
        total = share(half_t - s + 1 if d > 0 else s - half_t, c)
        if s > 1:
            rs_wait(s - 1, d, c)
            total = total + rs_in[rs_slot(s - 1, d, c)].astype(F32)
        slot = rs_slot(s, d, c)
        rs_out[slot] = total.astype(BF)
        copies.send(
            rs_out.at[slot], rs_in.at[slot], sem_rs[s, d, c], {"tp": (t + d + n_tp) % n_tp}
        )

    def rs_step(s):
        for c in range(SPLIT):
            rs_send(s, 1, c)
            if s < half_t:
                rs_send(s, -1, c)

    sem_ctx = copies.take(CTX)

    def to_tokens():
        totals = []
        for c in range(SPLIT):
            rs_wait(half_t, 1, c)
            total = share(0, c) + rs_in[rs_slot(half_t, 1, c)].astype(F32)
            if half_t > 1:
                rs_wait(half_t - 1, -1, c)
                total = total + rs_in[rs_slot(half_t - 1, -1, c)].astype(F32)
            total = total.astype(BF)
            totals += [total[:, j * quarter : (j + 1) * quarter] for j in range(wide // quarter)]
        stacked = jnp.concatenate(totals, axis=0)
        want = jnp.sum(jnp.where(line == t, table, 0.0), axis=0, keepdims=True)
        want = jnp.broadcast_to(want, (128, 128)).T[:, 0:64]
        pick = jnp.where((iota((128, 64), 1) + 1).astype(F32) == want, 1.0, 0.0).astype(BF)
        spread = dot(pick, stacked).astype(BF)
        for i in range(CTX):
            xs[i] = spread[16 * i : 16 * i + 16]
        for d in range(1, CTX):
            to = (ctx + d) % CTX
            copies.send(
                xs.at[(to % 2) * CHIPS + to // 2], xr.at[ctx], sem_ctx + d, {"ctx": to}
            )

    def tokens_out():
        total = xs[place].astype(F32)
        for d in range(1, CTX):
            source = (ctx - d + CTX) % CTX
            copies.arrived(xr.at[source], sem_ctx + d, {"ctx": source})
        for d in range(1, CTX):
            total = total + xr[(ctx - d + CTX) % CTX].astype(F32)
        for j in range(4):
            tok_ref[:, j * quarter : (j + 1) * quarter] = total[4 * j : 4 * j + 4].astype(BF)

    acc[...] = jnp.zeros_like(acc)
    if n_tp * CTX * CAP < 128:
        xc[...] = jnp.zeros_like(xc)

    def replicas(*offsets):
        numbers = [(z + o + n_dp) % n_dp for o in offsets]
        for i, b in enumerate(numbers):
            tab = hb[b, 3 * units :, :].astype(F32)
            for r in range(n_tp):
                got = dot(choosing(tab, r), g2[r * CTX : (r + 1) * CTX, b].reshape(128, 128))
                got = got.astype(BF)
                row = 128 * i + 16 * r
                for h in range(2):
                    for q in range(2):
                        at = (2 * h + q) * 16
                        xc[q, row : row + 16, 128 * h : 128 * h + 128] = got[at : at + 16]
        used = 128 * len(numbers)
        for q, first, count in ((0, 0, 2 * units), (1, 2 * units, units)):
            rows = [hb[b, first : first + count, :] for b in numbers]
            acc[first : first + count, :] += dot(jnp.concatenate(rows, axis=1), xc[q, 0:used])

    def all_from_sibling():
        for o in b2.offsets():
            a2.from_sibling(o)
            b2.from_sibling(o)

    plan = {s: [] for s in range(1, half_z + 1)}

    def at(s, *tasks):
        plan[min(s, half_z)] += tasks

    for s in range(b2_steps + 1, half_t + 1):
        at(s - b2_steps, functools.partial(b2.step, s), functools.partial(b2.along, s))
    for s in range(1, half_t + 1):
        at(s, functools.partial(a2.step, s))
        at(s + RS_AT, functools.partial(rs_step, s))
    for s in range(half_t + 1):
        at(max(s, 1) + 1, functools.partial(b2.onward, s))
        at(max(s, 1) + 2, functools.partial(b2.to_sibling, s))
    at(half_t + 2, all_from_sibling)
    at(half_t + 1 + RS_AT, to_tokens)
    at(half_t + 3 + RS_AT, tokens_out)
    ready = min(half_t + 2, half_z)
    waiting = [(0,)]
    for s in range(1, half_z + 1):
        last = s == half_z
        for task in plan[s]:
            task()
        for c in pieces:
            for d in (1, -1):
                ring_wait(half_z if last else -d * s, s, d, c)
                if not last:
                    ring_send(-d * s, s + 1, d, c)
            if s >= ready and waiting:
                replicas(*waiting.pop(0))
        waiting.append((-s, s) if not last else (half_z,))
    for offsets in waiting:
        replicas(*offsets)
    gate_ref[...] = acc[0:units, :] * scale
    up_ref[...] = acc[units : 2 * units, :] * scale
    down_ref[...] = acc[2 * units :, :] * scale
    copies.drain()


def sem_count(n_dp, n_tp):
    rows = 2 * (n_tp // 2)
    chips_first = 2 * (CHIPS + CHIPS * rows + n_tp)
    rows_first = rows + 4 * n_tp
    return chips_first + 2 * rows_first + n_dp + n_dp * PIECES + rows * SPLIT + CTX


def local(tokens, out_grad, expert_ids, gates, gate_proj, up_proj, down_proj):
    n_dp, n_tp = lax.axis_size("dp"), lax.axis_size("tp")
    width, units = tokens.shape[1], gate_proj.shape[1]
    quarter = width // 4
    devices = n_tp * CTX
    scale = 1.0 / math.sqrt(tokens.shape[0] * n_dp * devices)
    routing = jnp.concatenate([expert_ids.T.astype(F32), gates.T.astype(F32)], axis=0)
    routing = jnp.pad(routing, ((0, 4), (0, width - TOK)))
    xd = jnp.concatenate([tokens.astype(F32), out_grad.astype(F32), routing], axis=0)
    vmem = pl.BlockSpec(memory_space=pltpu.VMEM)
    hbm = pl.BlockSpec(memory_space=pl.ANY)
    grad = jax.ShapeDtypeStruct((units, width // n_dp), F32)
    sems = sem_count(n_dp, n_tp)
    token_grad, gate_grad, up_grad, down_grad = pl.pallas_call(
        functools.partial(kernel, (n_dp, n_tp, width, units, scale)),
        out_shape=(jax.ShapeDtypeStruct(tokens.shape, BF), grad, grad, grad),
        in_specs=[vmem, hbm, hbm, hbm],
        out_specs=(vmem, vmem, vmem, vmem),
        scratch_shapes=[
            pltpu.VMEM((devices, ROWS, quarter + 128), BF),
            pltpu.VMEM((devices, ROWS, quarter), BF),
            pltpu.VMEM((devices, n_dp, ROWS, 128), BF),
            pltpu.VMEM((n_dp, ROWS, 128), BF),
            pltpu.VMEM((2 * units, width), BF),
            pltpu.VMEM((units, width), BF),
            pltpu.VMEM((128, width), BF),
            pltpu.VMEM((128, width), BF),
            pltpu.VMEM((n_dp, 3 * units + ROWS, 128), BF),
            pltpu.VMEM((2, 256, 256), BF),
            pltpu.VMEM((3 * units, 256), F32),
            pltpu.VMEM((128, width), F32),
            pltpu.VMEM((n_tp * SPLIT, 16, width // SPLIT), BF),
            pltpu.VMEM((n_tp * SPLIT, 16, width // SPLIT), BF),
            pltpu.VMEM((CTX, ROWS, quarter), BF),
            pltpu.VMEM((CTX, ROWS, quarter), BF),
            pltpu.SemaphoreType.DMA((sems,)),
            pltpu.SemaphoreType.DMA((sems,)),
            pltpu.SemaphoreType.DMA((3,)),
        ],
        compiler_params=pltpu.CompilerParams(
            collective_id=0, has_side_effects=True, vmem_limit_bytes=52 * 2**20
        ),
    )(
        xd,
        gate_proj[0],
        up_proj[0],
        down_proj[0],
    )
    return token_grad, gate_grad[None], up_grad[None], down_grad[None]


def solution(mesh):
    rows = P(("dp", "ctx", "tp"), None)
    weights = P("ctx", "tp", None)
    grads = P("ctx", "tp", "dp")
    return jax.shard_map(
        local,
        mesh=mesh,
        in_specs=(rows, rows, rows, rows, weights, weights, weights),
        out_specs=(rows, grads, grads, grads),
        check_vma=False,
    )
```

```python
import functools
import math

import jax
import jax.numpy as jnp
from jax import lax
from jax.experimental import pallas as pl
from jax.experimental.pallas import tpu as pltpu
from jax.sharding import PartitionSpec as P

BF = jnp.bfloat16
F32 = jnp.float32
CHIPS = 4
CTX = 8
TOK = 4
CAP = 2
PIECES = 4
DRAIN = 32
RS_AT = 2
SPLIT = 2
ROWS = 16


def dot(a, b):
    return jnp.dot(a, b, preferred_element_type=F32)


def dot_t(a, b):
    return lax.dot_general(a, b, (((1,), (1,)), ((), ())), preferred_element_type=F32)


def iota(shape, dim):
    return lax.broadcasted_iota(jnp.int32, shape, dim)


class Copies:
    def __init__(self, send_sems, recv_sems):
        self.send_sems, self.recv_sems = send_sems, recv_sems
        self.used = 0
        self.sent = []

    def take(self, count=1):
        self.used += count
        return self.used - count

    def make(self, src, dst, sem, device):
        return pltpu.make_async_remote_copy(
            src_ref=src,
            dst_ref=dst,
            send_sem=self.send_sems.at[sem],
            recv_sem=self.recv_sems.at[sem],
            device_id=device,
            device_id_type=pl.DeviceIdType.MESH,
        )

    def send(self, src, dst, sem, device):
        copy = self.make(src, dst, sem, device)
        copy.start()
        self.sent.append(copy)

    def arrived(self, ref, sem, device):
        self.make(ref, ref, sem, device).wait_recv()

    def drain(self, count=None):
        count = len(self.sent) if count is None else count
        for copy in self.sent[:count]:
            copy.wait_send()
        self.sent = self.sent[count:]


class Plane:
    def __init__(self, copies, n_tp):
        self.c, self.n, self.half = copies, n_tp, n_tp // 2
        ctx, self.t = lax.axis_index("ctx"), lax.axis_index("tp")
        self.x, self.k = ctx // 2, ctx % 2
        self.sibling = {"ctx": 2 * self.x + 1 - self.k}

    def offsets(self):
        return list(range(-(self.half - 1), self.half + 1))

    def row(self, o):
        return (self.t + o + self.n) % self.n

    def chip(self, d):
        return (self.x + d + CHIPS) % CHIPS

    def at_chip(self, d):
        return {"ctx": 2 * self.chip(d) + self.k}

    def at_row(self, d):
        return {"tp": self.row(d)}

    def block(self, o, d):
        return self.row(o) * CTX + self.k * CHIPS + self.chip(d)

    def four(self, o, core):
        return self.row(o) * CTX + core * CHIPS

    def at_step(self, s):
        return [0] if s == 0 else [-s, s] if s < self.half else [self.half]


class ChipsFirst(Plane):
    def __init__(self, copies, n_tp, ref, grouped=False):
        super().__init__(copies, n_tp)
        self.ref, self.grouped = ref, grouped
        self.sem_x = [copies.take() for _ in range(CHIPS)]
        self.sem_y = {
            (s, d, e): copies.take()
            for s in range(1, self.half + 1)
            for d in (1, -1)
            for e in range(CHIPS)
            if self.goes(s, d, e)
        }
        self.sem_s = {o: copies.take() for o in self.offsets()}

    def goes(self, s, d, e):
        if self.grouped:
            return e == 0
        return s < self.half or (e < 2) == (d > 0)

    def piece(self, o, s, d, e):
        if not self.grouped:
            return self.ref(self.block(o, -e), 1)
        if s < self.half:
            return self.ref(self.four(o, self.k), 4)
        return self.ref(self.four(o, self.k) + (0 if d > 0 else 2), 2)

    def send(self, o, s, d, e):
        if self.goes(s, d, e):
            ref = self.piece(o, s, d, e)
            self.c.send(ref, ref, self.sem_y[s, d, e], self.at_row(d))

    def wait(self, o, s, d, e):
        if self.goes(s, d, e):
            ref = self.piece(o, s, d, e)
            self.c.arrived(ref, self.sem_y[s, d, e], self.at_row(-d))

    def begin(self):
        own = self.ref(self.block(0, 0), 1)
        for d in (1, 3, 2):
            self.c.send(own, own, self.sem_x[d], self.at_chip(d))
        if not self.grouped:
            self.send(0, 1, 1, 0)
            self.send(0, 1, -1, 0)

    def rows_begin(self):
        for e in (1, 3, 2):
            self.c.arrived(self.ref(self.block(0, -e), 1), self.sem_x[e], self.at_chip(-e))
            if not self.grouped:
                self.send(0, 1, 1, e)
                self.send(0, 1, -1, e)
        if self.grouped:
            self.send(0, 1, 1, 0)
            self.send(0, 1, -1, 0)
        self.to_sibling(0)

    def step(self, s):
        last = s == self.half
        for e in (0, 1, 3, 2):
            self.wait(self.half if last else -s, s, 1, e)
            if not last:
                self.send(-s, s + 1, 1, e)
            self.wait(self.half if last else s, s, -1, e)
            if not last:
                self.send(s, s + 1, -1, e)
        for o in self.at_step(s):
            self.to_sibling(o)

    def to_sibling(self, o):
        ref = self.ref(self.four(o, self.k), 4)
        self.c.send(ref, ref, self.sem_s[o], self.sibling)

    def from_sibling(self, o):
        self.c.arrived(self.ref(self.four(o, 1 - self.k), 4), self.sem_s[o], self.sibling)


class RowsFirst(Plane):
    def __init__(self, copies, n_tp, ref, split):
        super().__init__(copies, n_tp)
        self.ref, self.split = ref, split
        steps = range(1, self.half + 1)
        self.sem_y = {(s, d): copies.take() for s in steps for d in (1, -1)}
        self.sem_x = {(o, d): copies.take() for o in self.offsets() for d in (1, -1)}
        self.sem_f = {o: copies.take() for o in self.offsets()}
        self.sem_s = {o: copies.take() for o in self.offsets()}

    def part(self, o, s, d):
        at = self.block(o, 0)
        return self.ref(at, 1) if s < self.half else self.split(at, 0 if d > 0 else 1)

    def send(self, o, s, d):
        ref = self.part(o, s, d)
        self.c.send(ref, ref, self.sem_y[s, d], self.at_row(d))

    def wait(self, o, s, d):
        self.c.arrived(self.part(o, s, d), self.sem_y[s, d], self.at_row(-d))

    def begin(self):
        self.send(0, 1, 1)
        self.send(0, 1, -1)

    def step(self, s):
        last = s == self.half
        self.wait(self.half if last else -s, s, 1)
        if not last:
            self.send(-s, s + 1, 1)
        self.wait(self.half if last else s, s, -1)
        if not last:
            self.send(s, s + 1, -1)

    def along(self, s):
        for o in self.at_step(s):
            ref = self.ref(self.block(o, 0), 1)
            for d in (1, -1):
                self.c.send(ref, ref, self.sem_x[o, d], self.at_chip(d))

    def turn(self, o):
        return 1 if o <= 0 else -1

    def onward(self, s):
        for o in self.at_step(s):
            for d in (1, -1):
                self.c.arrived(self.ref(self.block(o, -d), 1), self.sem_x[o, d], self.at_chip(-d))
            d = self.turn(o)
            ref = self.ref(self.block(o, -d), 1)
            self.c.send(ref, ref, self.sem_f[o], self.at_chip(d))

    def to_sibling(self, s):
        for o in self.at_step(s):
            d = self.turn(o)
            self.c.arrived(self.ref(self.block(o, 2), 1), self.sem_f[o], self.at_chip(-d))
            ref = self.ref(self.four(o, self.k), 4)
            self.c.send(ref, ref, self.sem_s[o], self.sibling)

    def from_sibling(self, o):
        self.c.arrived(self.ref(self.four(o, 1 - self.k), 4), self.sem_s[o], self.sibling)


def kernel(
    sizes, xd_ref, routing_ref, gate_hbm, up_hbm, down_hbm,
    tok_ref, gate_ref, up_ref, down_ref,
    ga, gb, g2, zp, wgu, wd, rx, rd, hb, xc, acc, part, rs_in, rs_out, xs, xr,
    send_sems, recv_sems, load_sems,
):
    n_dp, n_tp, width, units, scale = sizes
    quarter = width // 4
    half_z, half_t = n_dp // 2, n_tp // 2
    z, ctx, t = lax.axis_index("dp"), lax.axis_index("ctx"), lax.axis_index("tp")
    place = (ctx % 2) * CHIPS + ctx // 2
    me = t * CTX + place

    barrier = pltpu.get_barrier_semaphore()
    for d in range(1, n_dp):
        pl.semaphore_signal(
            barrier, inc=1, device_id={"dp": (z + d) % n_dp}, device_id_type=pl.DeviceIdType.MESH
        )
    for d in range(1, CTX):
        pl.semaphore_signal(
            barrier, inc=1, device_id={"ctx": (ctx + d) % CTX}, device_id_type=pl.DeviceIdType.MESH
        )
    rows = (1, -1) if n_tp > 2 else (1,)
    for d in rows:
        pl.semaphore_signal(
            barrier,
            inc=1,
            device_id={"tp": (t + d + n_tp) % n_tp},
            device_id_type=pl.DeviceIdType.MESH,
        )
    loads = [
        pltpu.make_async_copy(gate_hbm, wgu.at[pl.ds(0, units)], load_sems.at[0]),
        pltpu.make_async_copy(up_hbm, wgu.at[pl.ds(units, units)], load_sems.at[1]),
        pltpu.make_async_copy(down_hbm, wd, load_sems.at[2]),
    ]
    for load in loads:
        load.start()

    def stacked_rows(first, size):
        halves = [xd_ref[0:8, at : at + size] for at in (first, first + size)]
        return jnp.concatenate(halves, axis=0).astype(BF)

    ga[me, :, 0:quarter] = stacked_rows(0, quarter)
    gb[me] = stacked_rows(2 * quarter, quarter)
    for i in range(n_dp):
        zp[i] = stacked_rows(256 * i, 128)
    g2[me, z] = zp[z]
    line, lane = iota((ROWS, 128), 0), iota((ROWS, 128), 1)
    expert = (line % 8).astype(F32)
    inner = lane % ROWS
    first = ((inner // 4) * 16 + 2 * place + 1).astype(F32)
    is_grad = (inner // 4) % 2 == 1
    count = jnp.zeros((ROWS, 128), F32)
    meta = jnp.zeros((ROWS, 128), F32)
    routing = routing_ref[...]
    for n in range(TOK):
        named, coefficient = line < 0, jnp.zeros((ROWS, 128), F32)
        for k in range(2):
            chosen = expert == routing[k : k + 1, n : n + 1]
            named = named | chosen
            coefficient = jnp.where(chosen, routing[k + 2 : k + 3, n : n + 1], coefficient)
        factor = jnp.where(is_grad, coefficient, 1.0)
        value = jnp.where(line < 8, first + count, factor)
        meta = jnp.where(named & (inner % 4 == n) & (lane // ROWS == place), value, meta)
        count = count + jnp.where(named, 1.0, 0.0)
    ga[me, :, quarter:] = meta.astype(BF)

    pl.semaphore_wait(barrier, n_dp - 1 + CTX - 1 + len(rows))

    copies = Copies(send_sems, recv_sems)
    a1 = ChipsFirst(copies, n_tp, lambda at, size: ga.at[pl.ds(at, size)])
    b1 = RowsFirst(
        copies,
        n_tp,
        lambda at, size: gb.at[pl.ds(at, size)],
        lambda at, part: gb.at[pl.ds(at, 1), :, pl.ds(part * (quarter // 2), quarter // 2)],
    )
    low = n_dp // 2
    a2 = ChipsFirst(copies, n_tp, lambda at, size: g2.at[pl.ds(at, size), pl.ds(0, low)], grouped=True)
    b2 = RowsFirst(
        copies,
        n_tp,
        lambda at, size: g2.at[pl.ds(at, size), pl.ds(low, low)],
        lambda at, part: g2.at[pl.ds(at, 1), pl.ds(low + part * (low // 2), low // 2)],
    )
    sem_z = copies.take(n_dp)

    def columns_send():
        for d in range(1, n_dp):
            to = (z + d) % n_dp
            copies.send(zp.at[to], g2.at[me, z], sem_z + d, {"dp": to})

    def columns_begin():
        for d in range(1, n_dp):
            source = (z - d + n_dp) % n_dp
            copies.arrived(g2.at[me, source], sem_z + d, {"dp": source})
        b2.begin()
        b2.along(0)
        a2.begin()

    begin_at = min(2, half_t)
    b1.begin()
    a1.begin()
    b1.along(0)
    columns_send()
    b1.step(1)
    b1.along(1)
    a1.rows_begin()
    b2_steps = 0
    for s in range(1, half_t + 1):
        if s < half_t:
            b1.step(s + 1)
            b1.along(s + 1)
        b1.onward(s - 1)
        if s == half_t:
            b1.onward(s)
        if s > 1:
            b1.to_sibling(s - 2)
        if s == begin_at:
            columns_begin()
        elif s > begin_at:
            b2_steps += 1
            b2.step(b2_steps)
            b2.along(b2_steps)
        a1.step(s)
    b1.to_sibling(half_t - 1)
    b1.to_sibling(half_t)
    if b2_steps + 1 < half_t:
        b2_steps += 1
        b2.step(b2_steps)
        b2.along(b2_steps)
    a2.rows_begin()
    for o in a1.offsets():
        a1.from_sibling(o)
        b1.from_sibling(o)
    for load in loads:
        load.wait()

    table = jnp.zeros((ROWS, 128), F32)
    for r in range(n_tp):
        total = ga[r * CTX, :, quarter:].astype(F32)
        for i in range(1, CTX):
            total = total + ga[r * CTX + i, :, quarter:].astype(F32)
        slot = jnp.sum(jnp.where(line == ctx, total, 0.0), axis=0, keepdims=True)
        factor = jnp.sum(jnp.where(line == 8 + ctx, total, 0.0), axis=0, keepdims=True)
        table = table + jnp.where(line == r, slot, 0.0) + jnp.where(line == 8 + r, factor, 0.0)
    hb[z, 3 * units :, :] = table.astype(BF)

    def choosing(tab, r):
        want = tab[r : r + 1, :]
        value = tab[8 + r : 9 + r, :]
        number = (iota((64, 128), 0) + 1).astype(F32)
        return jnp.where(number == want, value, 0.0).astype(BF)

    if n_tp * CTX * CAP < 128:
        rx[...] = jnp.zeros_like(rx)
        rd[...] = jnp.zeros_like(rd)
    for r in range(n_tp):
        pick = choosing(table, r)
        for side, block in enumerate((ga, gb)):
            got = dot(pick, block[r * CTX : (r + 1) * CTX, :, 0:quarter].reshape(128, quarter))
            got = got.astype(BF)
            for h in range(2):
                at = (2 * side + h) * quarter
                rx[16 * r : 16 * r + 16, at : at + quarter] = got[32 * h : 32 * h + 16]
                rd[16 * r : 16 * r + 16, at : at + quarter] = got[32 * h + 16 : 32 * h + 32]
    both = dot_t(wgu[:, 0:quarter], rx[:, 0:quarter])
    d_hidden = dot_t(wd[:, 0:quarter], rd[:, 0:quarter])
    for j in range(1, 4):
        cols = slice(j * quarter, (j + 1) * quarter)
        both = both + dot_t(wgu[:, cols], rx[:, cols])
        d_hidden = d_hidden + dot_t(wd[:, cols], rd[:, cols])
    pre_gate, pre_up = both[:units], both[units:]
    sigmoid = 1.0 / (1.0 + jnp.exp(-pre_gate))
    activated = pre_gate * sigmoid
    d_up = d_hidden * activated
    d_gate = d_hidden * pre_up * (sigmoid * (1.0 + pre_gate * (1.0 - sigmoid)))
    hb[z, 0:units, :] = d_gate.astype(BF)
    hb[z, units : 2 * units, :] = d_up.astype(BF)
    hb[z, 2 * units : 3 * units, :] = (activated * pre_up).astype(BF)

    lines = 3 * units + ROWS
    cuts = [lines * c // (16 * PIECES) * 16 for c in range(PIECES + 1)]
    pieces = range(PIECES)

    def ring_goes(s, d, c):
        return s < half_z or (c < PIECES // 2) == (d > 0)

    sem_ring = {
        (s, d, c): copies.take()
        for s in range(1, half_z + 1)
        for d in (1, -1)
        for c in pieces
        if ring_goes(s, d, c)
    }

    def ring_part(o, c):
        return hb.at[(z + o + n_dp) % n_dp, pl.ds(cuts[c], cuts[c + 1] - cuts[c])]

    def ring_send(o, s, d, c):
        if ring_goes(s, d, c):
            ref = ring_part(o, c)
            copies.send(ref, ref, sem_ring[s, d, c], {"dp": (z + d + n_dp) % n_dp})

    def ring_wait(o, s, d, c):
        if ring_goes(s, d, c):
            copies.arrived(ring_part(o, c), sem_ring[s, d, c], {"dp": (z - d + n_dp) % n_dp})

    for c in pieces:
        ring_send(0, 1, 1, c)
        ring_send(0, 1, -1, c)

    by_slot = jnp.concatenate([d_gate, d_up], axis=0).T.astype(BF)
    step_cols = min(512, width)

    @pl.loop(0, width // step_cols)
    def _(i):
        cols = pl.ds(pl.multiple_of(i * step_cols, step_cols), step_cols)
        part[:, cols] = dot(by_slot, wgu[:, cols])

    wide = width // SPLIT
    sem_rs = {
        (s, d, c): copies.take() for s in range(1, half_t + 1) for d in (1, -1) for c in range(SPLIT)
    }

    def share(o, c):
        at = pl.multiple_of((t + o + n_tp) % n_tp * 16, 16)
        return part[pl.ds(at, 16), c * wide : (c + 1) * wide]

    def rs_slot(s, d, c):
        return (s - 1 if d > 0 else half_t + s - 1) * SPLIT + c

    def rs_wait(s, d, c):
        ref = rs_in.at[rs_slot(s, d, c)]
        copies.arrived(ref, sem_rs[s, d, c], {"tp": (t - d + n_tp) % n_tp})

    def rs_send(s, d, c):
        total = share(half_t - s + 1 if d > 0 else s - half_t, c)
        if s > 1:
            rs_wait(s - 1, d, c)
            total = total + rs_in[rs_slot(s - 1, d, c)].astype(F32)
        slot = rs_slot(s, d, c)
        rs_out[slot] = total.astype(BF)
        copies.send(
            rs_out.at[slot], rs_in.at[slot], sem_rs[s, d, c], {"tp": (t + d + n_tp) % n_tp}
        )

    def rs_step(s):
        for c in range(SPLIT):
            rs_send(s, 1, c)
            if s < half_t:
                rs_send(s, -1, c)

    sem_ctx = copies.take(CTX)

    def to_tokens():
        totals = []
        for c in range(SPLIT):
            rs_wait(half_t, 1, c)
            total = share(0, c) + rs_in[rs_slot(half_t, 1, c)].astype(F32)
            if half_t > 1:
                rs_wait(half_t - 1, -1, c)
                total = total + rs_in[rs_slot(half_t - 1, -1, c)].astype(F32)
            total = total.astype(BF)
            totals += [total[:, j * quarter : (j + 1) * quarter] for j in range(wide // quarter)]
        stacked = jnp.concatenate(totals, axis=0)
        want = jnp.sum(jnp.where(line == t, table, 0.0), axis=0, keepdims=True)
        want = jnp.broadcast_to(want, (128, 128)).T[:, 0:64]
        pick = jnp.where((iota((128, 64), 1) + 1).astype(F32) == want, 1.0, 0.0).astype(BF)
        spread = dot(pick, stacked).astype(BF)
        for i in range(CTX):
            xs[i] = spread[16 * i : 16 * i + 16]
        for d in range(1, CTX):
            to = (ctx + d) % CTX
            copies.send(
                xs.at[(to % 2) * CHIPS + to // 2], xr.at[ctx], sem_ctx + d, {"ctx": to}
            )

    def tokens_out():
        total = xs[place].astype(F32)
        for d in range(1, CTX):
            source = (ctx - d + CTX) % CTX
            copies.arrived(xr.at[source], sem_ctx + d, {"ctx": source})
        for d in range(1, CTX):
            total = total + xr[(ctx - d + CTX) % CTX].astype(F32)
        for j in range(4):
            tok_ref[:, j * quarter : (j + 1) * quarter] = total[4 * j : 4 * j + 4].astype(BF)

    acc[...] = jnp.zeros_like(acc)
    if n_tp * CTX * CAP < 128:
        xc[...] = jnp.zeros_like(xc)

    def replicas(*offsets):
        numbers = [(z + o + n_dp) % n_dp for o in offsets]
        for i, b in enumerate(numbers):
            tab = hb[b, 3 * units :, :].astype(F32)
            for r in range(n_tp):
                got = dot(choosing(tab, r), g2[r * CTX : (r + 1) * CTX, b].reshape(128, 128))
                got = got.astype(BF)
                row = 128 * i + 16 * r
                for h in range(2):
                    for q in range(2):
                        at = (2 * h + q) * 16
                        xc[q, row : row + 16, 128 * h : 128 * h + 128] = got[at : at + 16]
        used = 128 * len(numbers)
        for q, first, count in ((0, 0, 2 * units), (1, 2 * units, units)):
            rows = [hb[b, first : first + count, :] for b in numbers]
            acc[first : first + count, :] += dot(jnp.concatenate(rows, axis=1), xc[q, 0:used])

    def all_from_sibling():
        for o in b2.offsets():
            a2.from_sibling(o)
            b2.from_sibling(o)

    plan = {s: [] for s in range(1, half_z + 1)}

    def at(s, *tasks):
        plan[min(s, half_z)] += tasks

    for s in range(half_t + 1):
        at(max(s, 1), functools.partial(b2.onward, s))
        at(max(s, 1) + 1, functools.partial(b2.to_sibling, s))
    for s in range(b2_steps + 1, half_t + 1):
        at(s - b2_steps, functools.partial(b2.step, s), functools.partial(b2.along, s))
    for s in range(1, half_t + 1):
        at(s, functools.partial(a2.step, s))
        at(s + RS_AT, functools.partial(rs_step, s))
    at(half_t + 2, all_from_sibling)
    at(half_t + 1 + RS_AT, to_tokens)
    at(half_t + 3 + RS_AT, tokens_out)
    ready = min(half_t + 2, half_z)
    waiting = [(0,)]
    for s in range(1, half_z + 1):
        last = s == half_z
        for task in plan[s]:
            task()
        for c in pieces:
            for d in (1, -1):
                ring_wait(half_z if last else -d * s, s, d, c)
                if not last:
                    ring_send(-d * s, s + 1, d, c)
            if s >= ready and waiting:
                replicas(*waiting.pop(0))
        if 1 < s < half_z:
            copies.drain(DRAIN)
        waiting.append((-s, s) if not last else (half_z,))
    for offsets in waiting:
        replicas(*offsets)
    gate_ref[...] = acc[0:units, :] * scale
    up_ref[...] = acc[units : 2 * units, :] * scale
    down_ref[...] = acc[2 * units :, :] * scale
    copies.drain()


def sem_count(n_dp, n_tp):
    rows = 2 * (n_tp // 2)
    chips_first = 2 * (CHIPS + CHIPS * rows + n_tp)
    rows_first = rows + 4 * n_tp
    return chips_first + 2 * rows_first + n_dp + n_dp * PIECES + rows * SPLIT + CTX


def local(tokens, out_grad, expert_ids, gates, gate_proj, up_proj, down_proj):
    n_dp, n_tp = lax.axis_size("dp"), lax.axis_size("tp")
    width, units = tokens.shape[1], gate_proj.shape[1]
    quarter = width // 4
    devices = n_tp * CTX
    scale = 1.0 / math.sqrt(tokens.shape[0] * n_dp * devices)
    xd = jnp.concatenate([tokens, out_grad], axis=0).astype(F32)
    routing = jnp.concatenate([expert_ids.T.astype(BF), gates.T], axis=0).astype(F32)
    vmem = pl.BlockSpec(memory_space=pltpu.VMEM)
    hbm = pl.BlockSpec(memory_space=pl.ANY)
    grad = jax.ShapeDtypeStruct((units, width // n_dp), F32)
    sems = sem_count(n_dp, n_tp)
    token_grad, gate_grad, up_grad, down_grad = pl.pallas_call(
        functools.partial(kernel, (n_dp, n_tp, width, units, scale)),
        out_shape=(jax.ShapeDtypeStruct(tokens.shape, BF), grad, grad, grad),
        in_specs=[vmem, vmem, hbm, hbm, hbm],
        out_specs=(vmem, vmem, vmem, vmem),
        scratch_shapes=[
            pltpu.VMEM((devices, ROWS, quarter + 128), BF),
            pltpu.VMEM((devices, ROWS, quarter), BF),
            pltpu.VMEM((devices, n_dp, ROWS, 128), BF),
            pltpu.VMEM((n_dp, ROWS, 128), BF),
            pltpu.VMEM((2 * units, width), BF),
            pltpu.VMEM((units, width), BF),
            pltpu.VMEM((128, width), BF),
            pltpu.VMEM((128, width), BF),
            pltpu.VMEM((n_dp, 3 * units + ROWS, 128), BF),
            pltpu.VMEM((2, 256, 256), BF),
            pltpu.VMEM((3 * units, 256), F32),
            pltpu.VMEM((128, width), F32),
            pltpu.VMEM((n_tp * SPLIT, 16, width // SPLIT), BF),
            pltpu.VMEM((n_tp * SPLIT, 16, width // SPLIT), BF),
            pltpu.VMEM((CTX, ROWS, quarter), BF),
            pltpu.VMEM((CTX, ROWS, quarter), BF),
            pltpu.SemaphoreType.DMA((sems,)),
            pltpu.SemaphoreType.DMA((sems,)),
            pltpu.SemaphoreType.DMA((3,)),
        ],
        compiler_params=pltpu.CompilerParams(
            collective_id=0, has_side_effects=True, vmem_limit_bytes=52 * 2**20
        ),
    )(
        xd,
        routing,
        gate_proj[0],
        up_proj[0],
        down_proj[0],
    )
    return token_grad, gate_grad[None], up_grad[None], down_grad[None]


def solution(mesh):
    rows = P(("dp", "ctx", "tp"), None)
    weights = P("ctx", "tp", None)
    grads = P("ctx", "tp", "dp")
    return jax.shard_map(
        local,
        mesh=mesh,
        in_specs=(rows, rows, rows, rows, weights, weights, weights),
        out_specs=(rows, grads, grads, grads),
        check_vma=False,
    )
```
